256 devices in a mesh: copy: 64 (over z_hi, y, x), tp: 4 (over z_lo, core).
Axes of the slice: x: 4, y: 4, z: 8 (z_hi: 4, z_lo: 2; z = z_hi * 2 + z_lo), core: 2. Of those that a mesh axis runs over, the one named last changes fastest.
Arguments:
- layer_inputs: bfloat16 [64, 6, 512, 4, 1024], P('copy', None, None, 'tp'), may hold values from -16 to 16
- output_grads: bfloat16 [64, 6, 512, 1024], P('copy', None, 'tp'), may hold values from -6 to 6
- value_weights: bfloat16 [64, 4, 1024, 1024], P('copy', 'tp'), may hold values from -16 to 16
Outputs:
- merged: bfloat16 [4, 1024, 1024], P('tp', 'copy')
- fisher_mean: float32 [4, 1024, 1024], P('tp', 'copy')
The draws below stay inside these ranges and needn't reach their ends.
All inputs are finite; a program needn't handle non-finite values.
Results may differ from the reference program's by a relative error of at most 0.001.
Values may be sent and summed in bfloat16 or wider, within the bound.
A program may use at most 128 MiB of HBM per device.

```python
import jax
import jax.numpy as jnp
from jax import lax

FEAT_GRP = 1024
MB = 6
TOK_MB = 512
KVD = 1024
COPIES = 64
N_TP = 4


def raised(result, own_key, source, target, shards_of, factor):
    owner, partner = [(jnp.arange(result.shape[position]) // (result.shape[position] // shards_of)).reshape([-1 if axis == position else 1 for axis in range(result.ndim)]) for position in (source, target)]
    chosen = jax.random.permutation(own_key, shards_of)[partner]
    strong = (owner == chosen) | (owner == (partner + shards_of // 2) % shards_of)
    return jnp.where(strong, factor * result, result)


def level_of(stream_key, shape, cuts, least, largest):
    def one(axis_at, parts):
        steps = jax.random.uniform(jax.random.fold_in(jax.random.fold_in(stream_key, 6), axis_at), (parts,), jnp.float32, least / len(cuts), largest / len(cuts))
        return jnp.repeat(jnp.exp(steps), shape[axis_at] // parts).reshape((-1,) + (1,) * (len(shape) - axis_at - 1))

    loudness = one(*cuts[0])
    for cut in cuts[1:]:
        loudness = loudness * one(*cut)
    return loudness


def scatter_about(rng, dims, deviation, reach, shards=(), held_as=jnp.bfloat16):
    result = deviation * jax.random.normal(rng, dims, jnp.float32)
    if shards:
        result = result * level_of(rng, dims, shards, -0.22, 0.18)
    return jnp.clip(result, -reach, reach).astype(held_as)


def heavy_noise(own_key, shape, deviation, most, cuts, heavy, dtype=jnp.bfloat16):
    values = deviation * jax.random.normal(own_key, shape, jnp.float32)
    if cuts:
        values = values * level_of(own_key, shape, cuts, -0.22, 0.18)
    return jnp.clip(raised(values, jax.random.fold_in(own_key, 3), *heavy), -most, most).astype(dtype)


def setup_inputs(seed: int = 0) -> dict:
    keys = jax.random.split(jax.random.key(seed), 4)
    return {
        "layer_inputs": heavy_noise(keys[0], (COPIES, MB, TOK_MB, N_TP, FEAT_GRP), 1.0, 16.0, ((0, 64), (3, 4)), (0, 4, 64, 4.0)),
        "output_grads": scatter_about(keys[1], (COPIES, MB, TOK_MB, KVD), 1.0, 6.0, ((0, 64), (2, 4))),
        "value_weights": heavy_noise(keys[2], (COPIES, N_TP, FEAT_GRP, KVD), 1.0, 16.0, ((0, 64), (1, 4)), (0, 2, 64, 4.0)),
    }


epsilon = 1e-6


def copy_fisher(inputs_copy, grads_copy):
    def accumulate(running, sample):
        inputs_mb, grads_mb = sample
        flat_inputs = inputs_mb.reshape(TOK_MB, N_TP * FEAT_GRP)
        gradient = jnp.dot(flat_inputs.T, grads_mb, preferred_element_type=jnp.float32)
        return running + gradient * gradient, None

    zero_grid = jnp.zeros((N_TP * FEAT_GRP, KVD), jnp.float32)
    fisher, _ = lax.scan(accumulate, zero_grid, (inputs_copy, grads_copy))
    return fisher / (MB * TOK_MB)


def reference(layer_inputs, output_grads, value_weights):
    def per_copy(running, sample):
        weighted, total = running
        inputs_copy, grads_copy, weights_copy = sample
        fisher = copy_fisher(inputs_copy, grads_copy)
        weights_flat = weights_copy.reshape(N_TP * FEAT_GRP, KVD).astype(jnp.float32)
        return (weighted + fisher * weights_flat, total + fisher), None

    zero_grid = jnp.zeros((N_TP * FEAT_GRP, KVD), jnp.float32)
    (weighted, total), _ = lax.scan(per_copy, (zero_grid, zero_grid), (layer_inputs, output_grads, value_weights))
    fisher_mean = (total / COPIES).reshape(N_TP, FEAT_GRP, KVD)
    merged = (weighted / (total + epsilon)).astype(jnp.bfloat16).reshape(N_TP, FEAT_GRP, KVD)
    return merged, fisher_mean
```

```python
import jax
import jax.numpy as jnp
from jax import lax
from jax.experimental import pallas as pl
from jax.experimental.pallas import tpu as pltpu
from jax.sharding import PartitionSpec as P

EPSILON = 1e-6
RING = 4
HALF = RING // 2
ROWS = 16
CW = 128
LAG1, LAG2, LAG3 = 2, 3, 4
MESH = pl.DeviceIdType.MESH


def kernel(x_hbm, g_hbm, w_hbm, merged_ref, mean_ref,
           xv, xt, g, wv, f, rwx, rwy, r1x, r1y, s2x, s2y, r2x, r2y, s3, r3,
           x_sem, g_sem, w_sem, send_sem, rz, rc, rr, rw, r1_sem, r2_sem, r3_sem):
    batches, tokens, features = x_hbm.shape
    own_tokens = g_hbm.shape[1]
    blocks = g.shape[0]
    copy, tp = lax.axis_index("copy"), lax.axis_index("tp")
    z, y, x = copy // 16, (copy // 4) % 4, copy % 4
    chip, core = tp // 2, tp % 2

    def turn(v, by):
        return lax.rem(v + by, RING)

    def at(zz, yy, xx):
        return (zz * 16 + yy * 4 + xx, tp)

    pair = (copy, (1 - chip) * 2 + core)
    sibling = (copy, chip * 2 + 1 - core)
    own_rows = pl.ds(pl.multiple_of(tp * own_tokens, own_tokens), own_tokens)
    pair_rows = pl.ds(pl.multiple_of(pair[1] * own_tokens, own_tokens), own_tokens)

    loads = []
    for k in range(blocks):
        loads.append(pltpu.make_async_copy(
            g_hbm.at[:, :, pl.ds(k * CW, CW)], g.at[k, :, own_rows, :], g_sem.at[k]))
    w_load = pltpu.make_async_copy(w_hbm, wv, w_sem)
    x_loads = [pltpu.make_async_copy(x_hbm.at[m], xv.at[m], x_sem.at[m]) for m in range(batches)]
    for load in loads:
        load.start()
    w_load.start()
    for load in x_loads:
        load.start()

    barrier = pltpu.get_barrier_semaphore()
    partners = [pair, sibling]
    for d in range(1, RING):
        partners += [at(z, y, turn(x, d)), at(z, turn(y, d), x), at(turn(z, d), y, x)]
    for partner in partners:
        pl.semaphore_signal(barrier, 1, device_id=partner, device_id_type=MESH)
    pl.semaphore_wait(barrier, len(partners))

    def send(src, dst, slot, recv, to):
        pltpu.make_async_remote_copy(src, dst, send_sem.at[slot], recv, device_id=to, device_id_type=MESH).start()

    def take(ref, sem):
        pltpu.make_async_copy(ref, ref, sem).wait()

    for k in range(blocks):
        loads[k].wait()
        own = g.at[k, :, own_rows, :]
        send(own, own, 0, rz.at[k], pair)
        send(own, own, 1, rc.at[k], sibling)
    w_load.wait()
    for d in range(1, RING):
        send(wv.at[pl.ds(0, HALF), :, turn(x, d)], rwx.at[d - 1], 3, rw.at[0], at(z, y, turn(x, d)))
        send(wv.at[pl.ds(HALF, HALF), turn(y, d)], rwy.at[d - 1], 3, rw.at[1], at(z, turn(y, d), x))

    for m in range(batches):
        x_loads[m].wait()

        def turn_tile(i, c, m=m):
            cols = pl.ds(pl.multiple_of(i * 256, 256), 256)
            xt[m, cols, :] = xv[m, :, cols].T
            return c

        lax.fori_loop(0, features // 256, turn_tile, 0)

    def relay(k):
        got = g.at[k, :, pair_rows, :]
        take(got, rz.at[k])
        send(got, got, 2, rr.at[k], sibling)

    def compute(k):
        got = g.at[k, :, own_rows, :]
        take(got, rc.at[k])
        take(got, rr.at[k])

        def tile(i, c):
            rows = pl.ds(pl.multiple_of(i * 256, 256), 256)
            total = None
            for m in range(batches):
                gradient = jnp.dot(xt[m, rows, :], g[k, m], preferred_element_type=jnp.float32)
                square = gradient * gradient
                total = square if total is None else total + square
            f[k, i] = total.reshape(RING, RING, ROWS, CW)
            return c

        lax.fori_loop(0, HALF, tile, 0)
        for d in range(1, RING):
            send(f.at[k, pl.ds(0, HALF), :, turn(x, d)], r1x.at[k, d - 1], 4, r1_sem.at[0, k],
                 at(z, y, turn(x, d)))
        lax.fori_loop(HALF, RING, tile, 0)
        for d in range(1, RING):
            send(f.at[k, pl.ds(HALF, HALF), turn(y, d)], r1y.at[k, d - 1], 5, r1_sem.at[1, k],
                 at(z, turn(y, d), x))

    def stage1(k):
        cols = pl.ds(pl.multiple_of(k * CW, CW), CW)

        def add(own_f, own_w, rf, rw_):
            fisher = own_f
            weighted = own_f * own_w.astype(jnp.float32)
            for d in range(RING - 1):
                fisher = fisher + rf[k, d]
                weighted = weighted + rf[k, d] * rw_[d, :, :, :, cols].astype(jnp.float32)
            return weighted, fisher

        take(r1x.at[k], r1_sem.at[0, k])
        weighted, fisher = add(f[k, pl.ds(0, HALF), :, x], wv[pl.ds(0, HALF), :, x, :, cols], r1x, rwx)
        s2x[k, :, 0] = weighted
        s2x[k, :, 1] = fisher
        for d in range(1, RING):
            send(s2x.at[k, :, :, turn(y, d)], r2x.at[k, d - 1], 6, r2_sem.at[0, k], at(z, turn(y, d), x))
        take(r1y.at[k], r1_sem.at[1, k])
        weighted, fisher = add(f[k, pl.ds(HALF, HALF), y], wv[pl.ds(HALF, HALF), y, :, :, cols], r1y, rwy)
        s2y[k, :, 0] = weighted
        s2y[k, :, 1] = fisher
        for d in range(1, RING):
            send(s2y.at[k, :, :, turn(x, d)], r2y.at[k, d - 1], 7, r2_sem.at[1, k], at(z, y, turn(x, d)))

    def stage2(k):
        take(r2x.at[k], r2_sem.at[0, k])
        s3[k, pl.ds(0, HALF)] = s2x[k, :, :, y] + r2x[k, 0] + r2x[k, 1] + r2x[k, 2]
        take(r2y.at[k], r2_sem.at[1, k])
        s3[k, pl.ds(HALF, HALF)] = s2y[k, :, :, x] + r2y[k, 0] + r2y[k, 1] + r2y[k, 2]
        for d in range(1, RING):
            send(s3.at[k, turn(z, d)], r3.at[k, d - 1], 8, r3_sem.at[k], at(turn(z, d), y, x))

    def stage3(k):
        cols = pl.ds(pl.multiple_of(k * CW, CW), CW)
        take(r3.at[k], r3_sem.at[k])
        sums = (s3[k, z] + r3[k, 0] + r3[k, 1] + r3[k, 2]) * (1.0 / (batches * tokens))
        mean_ref[:, cols] = sums[1] * (1.0 / (RING * RING * RING))
        merged_ref[:, cols] = (sums[0] / (sums[1] + EPSILON)).astype(jnp.bfloat16)

    def step(i, c):
        @pl.when(i < blocks)
        def _():
            relay(i)

        @pl.when(i == LAG1)
        def _():
            take(rwx, rw.at[0])
            take(rwy, rw.at[1])

        @pl.when(jnp.logical_and(i >= LAG1, i < blocks + LAG1))
        def _():
            stage1(i - LAG1)

        @pl.when(jnp.logical_and(i >= LAG2, i < blocks + LAG2))
        def _():
            stage2(i - LAG2)

        @pl.when(i >= LAG3)
        def _():
            stage3(i - LAG3)

        @pl.when(i < blocks)
        def _():
            compute(i)

        return c

    lax.fori_loop(0, blocks + LAG3, step, 0)

    own = g.at[:, :, own_rows, :]
    for slot in range(3):
        take(own, send_sem.at[slot])
    take(rwx, send_sem.at[3])
    take(rwy, send_sem.at[3])
    for slot, ref in ((4, r1x), (5, r1y), (6, r2x), (7, r2y), (8, r3)):
        take(ref, send_sem.at[slot])


def local(layer_inputs, output_grads, value_weights):
    _, batches, tokens, _, features = layer_inputs.shape
    own_tokens, columns = output_grads.shape[2:]
    blocks = columns // CW
    f32, bf16 = jnp.float32, jnp.bfloat16
    dma = pltpu.SemaphoreType.DMA
    vmem = pltpu.VMEM
    merged, mean = pl.pallas_call(
        kernel,
        out_shape=(jax.ShapeDtypeStruct((ROWS, columns), bf16), jax.ShapeDtypeStruct((ROWS, columns), f32)),
        in_specs=[pl.BlockSpec(memory_space=pl.ANY)] * 3,
        out_specs=(pl.BlockSpec(memory_space=pltpu.VMEM),) * 2,
        scratch_shapes=[
            vmem((batches, tokens, features), bf16),
            vmem((batches, features, tokens), bf16),
            vmem((blocks, batches, tokens, CW), bf16),
            vmem((RING, RING, RING, ROWS, columns), bf16),
            vmem((blocks, RING, RING, RING, ROWS, CW), f32),
            vmem((RING - 1, HALF, RING, ROWS, columns), bf16),
            vmem((RING - 1, HALF, RING, ROWS, columns), bf16),
            vmem((blocks, RING - 1, HALF, RING, ROWS, CW), f32),
            vmem((blocks, RING - 1, HALF, RING, ROWS, CW), f32),
            vmem((blocks, HALF, 2, RING, ROWS, CW), f32),
            vmem((blocks, HALF, 2, RING, ROWS, CW), f32),
            vmem((blocks, RING - 1, HALF, 2, ROWS, CW), f32),
            vmem((blocks, RING - 1, HALF, 2, ROWS, CW), f32),
            vmem((blocks, RING, 2, ROWS, CW), f32),
            vmem((blocks, RING - 1, 2, ROWS, CW), f32),
            dma((batches,)), dma((blocks,)), dma, dma((9,)),
            dma((blocks,)), dma((blocks,)), dma((blocks,)), dma((2,)),
            dma((2, blocks)), dma((2, blocks)), dma((blocks,)),
        ],
        compiler_params=pltpu.CompilerParams(
            collective_id=0, has_side_effects=True, vmem_limit_bytes=56 << 20
        ),
        cost_estimate=pl.CostEstimate(
            flops=2 * batches * tokens * features * columns, bytes_accessed=10 << 20, transcendentals=0
        ),
        name="fisher_merge",
    )(
        layer_inputs.reshape(batches, tokens, features),
        output_grads.reshape(batches, own_tokens, columns),
        value_weights.reshape(RING, RING, RING, ROWS, columns),
    )
    return merged[None], mean[None]


def solution(mesh):
    return jax.shard_map(
        local,
        mesh=mesh,
        in_specs=(
            P("copy", None, None, "tp", None),
            P("copy", None, "tp", None),
            P("copy", "tp", None, None),
        ),
        out_specs=(P("tp", "copy", None), P("tp", "copy", None)),
        check_vma=False,
    )
```

```python
import jax
import jax.numpy as jnp
from jax import lax
from jax.experimental import pallas as pl
from jax.experimental.pallas import tpu as pltpu
from jax.sharding import PartitionSpec as P

EPSILON = 1e-6
RING = 4
HALF = RING // 2
ROWS = 16
CW = 128
LAG1, LAG2, LAG3 = 3, 5, 10
MESH = pl.DeviceIdType.MESH


def kernel(x_hbm, g_hbm, w_hbm, out_ref,
           xv, xt, g, wv, f, rwx, rwy, r1x, r1y, s2x, s2y, r2x, r2y, s3, r3,
           x_sem, g_sem, w_sem, send_sem, rz, rc, rr, rw, r1_sem, r2_sem, r3_sem):
    batches, tokens, features = x_hbm.shape
    own_tokens = g_hbm.shape[1]
    blocks = g.shape[0]
    copy, tp = lax.axis_index("copy"), lax.axis_index("tp")
    z, y, x = copy // 16, (copy // 4) % 4, copy % 4
    chip, core = tp // 2, tp % 2

    def turn(v, by):
        return lax.rem(v + by, RING)

    def at(zz, yy, xx):
        return (zz * 16 + yy * 4 + xx, tp)

    pair = (copy, (1 - chip) * 2 + core)
    sibling = (copy, chip * 2 + 1 - core)
    own_rows = pl.ds(pl.multiple_of(tp * own_tokens, own_tokens), own_tokens)
    pair_rows = pl.ds(pl.multiple_of(pair[1] * own_tokens, own_tokens), own_tokens)

    barrier = pltpu.get_barrier_semaphore()
    partners = [pair, sibling]
    for d in range(1, RING):
        partners += [at(z, y, turn(x, d)), at(z, turn(y, d), x), at(turn(z, d), y, x)]
    for partner in partners:
        pl.semaphore_signal(barrier, 1, device_id=partner, device_id_type=MESH)

    loads = []
    for k in range(blocks):
        loads.append(pltpu.make_async_copy(
            g_hbm.at[:, :, pl.ds(k * CW, CW)], g.at[k, :, own_rows, :], g_sem.at[k]))
    w_load = pltpu.make_async_copy(w_hbm, wv, w_sem)
    x_loads = [pltpu.make_async_copy(x_hbm.at[m], xv.at[m], x_sem.at[m]) for m in range(batches)]
    for load in loads:
        load.start()
    w_load.start()
    for load in x_loads:
        load.start()

    pl.semaphore_wait(barrier, len(partners))

    def send(src, dst, slot, recv, to):
        pltpu.make_async_remote_copy(src, dst, send_sem.at[slot], recv, device_id=to, device_id_type=MESH).start()

    def take(ref, sem):
        pltpu.make_async_copy(ref, ref, sem).wait()

    for k in range(blocks):
        loads[k].wait()
        own = g.at[k, :, own_rows, :]
        send(own, own, 0, rz.at[k], pair)
        send(own, own, 1, rc.at[k], sibling)
    w_load.wait()
    for d in range(1, RING):
        send(wv.at[pl.ds(0, HALF), :, turn(x, d)], rwx.at[d - 1], 3, rw.at[0], at(z, y, turn(x, d)))
        send(wv.at[pl.ds(HALF, HALF), turn(y, d)], rwy.at[d - 1], 3, rw.at[1], at(z, turn(y, d), x))

    for m in range(batches):
        x_loads[m].wait()

        def turn_tile(i, c, m=m):
            cols = pl.ds(pl.multiple_of(i * 256, 256), 256)
            xt[m, cols, :] = xv[m, :, cols].T
            return c

        lax.fori_loop(0, features // 256, turn_tile, 0)

    def relay(k):
        got = g.at[k, :, pair_rows, :]
        take(got, rz.at[k])
        send(got, got, 2, rr.at[k], sibling)

    def compute(k):
        got = g.at[k, :, own_rows, :]
        take(got, rc.at[k])
        take(got, rr.at[k])

        def tile(i):
            rows = pl.ds(i * 512, 512)
            total = None
            for m in range(batches):
                gradient = jnp.dot(xt[m, rows, :], g[k, m], preferred_element_type=jnp.float32)
                square = gradient * gradient
                total = square if total is None else total + square
            f[k, pl.ds(i * HALF, HALF)] = total.reshape(HALF, RING, RING, ROWS, CW)

        tile(0)
        for d in range(1, RING):
            send(f.at[k, pl.ds(0, HALF), :, turn(x, d)], r1x.at[k, d - 1], 4, r1_sem.at[0, k],
                 at(z, y, turn(x, d)))
        tile(1)
        for d in range(1, RING):
            send(f.at[k, pl.ds(HALF, HALF), turn(y, d)], r1y.at[k, d - 1], 5, r1_sem.at[1, k],
                 at(z, turn(y, d), x))

    def stage1(k):
        cols = pl.ds(pl.multiple_of(k * CW, CW), CW)

        def add(own_f, own_w, rf, rw_):
            fisher = own_f
            weighted = own_f * own_w.astype(jnp.float32)
            for d in range(RING - 1):
                fisher = fisher + rf[k, d]
                weighted = weighted + rf[k, d] * rw_[d, :, :, :, cols].astype(jnp.float32)
            return weighted, fisher

        take(r1x.at[k], r1_sem.at[0, k])
        weighted, fisher = add(f[k, pl.ds(0, HALF), :, x], wv[pl.ds(0, HALF), :, x, :, cols], r1x, rwx)
        s2x[k, :, 0] = weighted
        s2x[k, :, 1] = fisher
        for d in range(1, RING):
            send(s2x.at[k, :, :, turn(y, d)], r2x.at[k, d - 1], 6, r2_sem.at[0, k], at(z, turn(y, d), x))
        take(r1y.at[k], r1_sem.at[1, k])
        weighted, fisher = add(f[k, pl.ds(HALF, HALF), y], wv[pl.ds(HALF, HALF), y, :, :, cols], r1y, rwy)
        s2y[k, :, 0] = weighted
        s2y[k, :, 1] = fisher
        for d in range(1, RING):
            send(s2y.at[k, :, :, turn(x, d)], r2y.at[k, d - 1], 7, r2_sem.at[1, k], at(z, y, turn(x, d)))

    def stage2(k):
        take(r2x.at[k], r2_sem.at[0, k])
        s3[k, pl.ds(0, HALF)] = s2x[k, :, :, y] + r2x[k, 0] + r2x[k, 1] + r2x[k, 2]
        take(r2y.at[k], r2_sem.at[1, k])
        s3[k, pl.ds(HALF, HALF)] = s2y[k, :, :, x] + r2y[k, 0] + r2y[k, 1] + r2y[k, 2]

    def send3(k):
        for d in range(1, RING):
            send(s3.at[k, turn(z, d)], r3.at[k, d - 1], 8, r3_sem.at[k], at(turn(z, d), y, x))

    def stage3(k):
        cols = pl.ds(pl.multiple_of(k * CW, CW), CW)
        take(r3.at[k], r3_sem.at[k])
        sums = (s3[k, z] + r3[k, 0] + r3[k, 1] + r3[k, 2]) * (1.0 / (batches * tokens))
        out_ref[:, :, cols] = sums

    def step(i, c):
        @pl.when(i < blocks)
        def _():
            relay(i)

        @pl.when(i == LAG1)
        def _():
            take(rwx, rw.at[0])
            take(rwy, rw.at[1])

        @pl.when(jnp.logical_and(i >= LAG1, i < blocks + LAG1))
        def _():
            stage1(i - LAG1)

        @pl.when(jnp.logical_and(i >= LAG2, i < blocks + LAG2))
        def _():
            stage2(i - LAG2)

        @pl.when(i == blocks)
        def _():
            lax.fori_loop(0, blocks - LAG2 + 1, lambda k, c: (send3(k), c)[1], 0)

        @pl.when(jnp.logical_and(i > blocks, i < blocks + LAG2))
        def _():
            send3(i - LAG2)

        @pl.when(i >= LAG3)
        def _():
            stage3(i - LAG3)

        @pl.when(i < blocks)
        def _():
            compute(i)

        return c

    lax.fori_loop(0, blocks + LAG3, step, 0)

    own = g.at[:, :, own_rows, :]
    for slot in range(3):
        take(own, send_sem.at[slot])
    take(rwx, send_sem.at[3])
    take(rwy, send_sem.at[3])
    for slot, ref in ((4, r1x), (5, r1y), (6, r2x), (7, r2y), (8, r3)):
        take(ref, send_sem.at[slot])


def local(layer_inputs, output_grads, value_weights):
    _, batches, tokens, _, features = layer_inputs.shape
    own_tokens, columns = output_grads.shape[2:]
    blocks = columns // CW
    f32, bf16 = jnp.float32, jnp.bfloat16
    dma = pltpu.SemaphoreType.DMA
    vmem = pltpu.VMEM
    sums = pl.pallas_call(
        kernel,
        out_shape=jax.ShapeDtypeStruct((2, ROWS, columns), f32),
        in_specs=[pl.BlockSpec(memory_space=pl.ANY)] * 3,
        out_specs=pl.BlockSpec(memory_space=pltpu.VMEM),
        scratch_shapes=[
            vmem((batches, tokens, features), bf16),
            vmem((batches, features, tokens), bf16),
            vmem((blocks, batches, tokens, CW), bf16),
            vmem((RING, RING, RING, ROWS, columns), bf16),
            vmem((blocks, RING, RING, RING, ROWS, CW), f32),
            vmem((RING - 1, HALF, RING, ROWS, columns), bf16),
            vmem((RING - 1, HALF, RING, ROWS, columns), bf16),
            vmem((blocks, RING - 1, HALF, RING, ROWS, CW), f32),
            vmem((blocks, RING - 1, HALF, RING, ROWS, CW), f32),
            vmem((blocks, HALF, 2, RING, ROWS, CW), f32),
            vmem((blocks, HALF, 2, RING, ROWS, CW), f32),
            vmem((blocks, RING - 1, HALF, 2, ROWS, CW), f32),
            vmem((blocks, RING - 1, HALF, 2, ROWS, CW), f32),
            vmem((blocks, RING, 2, ROWS, CW), f32),
            vmem((blocks, RING - 1, 2, ROWS, CW), f32),
            dma((batches,)), dma((blocks,)), dma, dma((9,)),
            dma((blocks,)), dma((blocks,)), dma((blocks,)), dma((2,)),
            dma((2, blocks)), dma((2, blocks)), dma((blocks,)),
        ],
        compiler_params=pltpu.CompilerParams(
            collective_id=0, has_side_effects=True, vmem_limit_bytes=56 << 20
        ),
        cost_estimate=pl.CostEstimate(
            flops=2 * batches * tokens * features * columns, bytes_accessed=10 << 20, transcendentals=0
        ),
        name="fisher_merge",
    )(
        layer_inputs.reshape(batches, tokens, features),
        output_grads.reshape(batches, own_tokens, columns),
        value_weights.reshape(RING, RING, RING, ROWS, columns),
    )
    weighted, total = sums[:1], sums[1:]
    return (weighted / (total + EPSILON)).astype(bf16), total / lax.axis_size("copy")


def solution(mesh):
    return jax.shard_map(
        local,
        mesh=mesh,
        in_specs=(
            P("copy", None, None, "tp", None),
            P("copy", None, "tp", None),
            P("copy", "tp", None, None),
        ),
        out_specs=(P("tp", "copy", None), P("tp", "copy", None)),
        check_vma=False,
    )
```

```python
import jax
import jax.numpy as jnp
from jax import lax
from jax.experimental import pallas as pl
from jax.experimental.pallas import tpu as pltpu
from jax.sharding import PartitionSpec as P

EPSILON = 1e-6
RING = 4
HALF = RING // 2
ROWS = 16
CW = 128
LAG1, LAG2, LAG3 = 3, 5, 10
MESH = pl.DeviceIdType.MESH


def spacing(high):
    return (high * (1.0 + 1.01 / 256)).astype(jnp.bfloat16).astype(jnp.float32) - high


def split(value):
    high = value.astype(jnp.bfloat16)
    near = high.astype(jnp.float32)
    part = (value - near) * pl.reciprocal(jnp.maximum(spacing(near), 1e-30), approx=True)
    return high, jnp.clip(jnp.floor(part * 16.0 + 8.0), 0.0, 15.0)


def joined(high, sixteenths):
    near = high.astype(jnp.float32)
    return near + (sixteenths - 7.5) * (spacing(near) * (1.0 / 16))


def kernel(x_hbm, g_hbm, w_hbm, out_ref,
           xv, xt, g, wv, f, e, rwx, rwy, r1x, r1y, s2x, s2y, r2x, r2y, s3, r3,
           x_sem, g_sem, w_sem, send_sem, rz, rc, rr, rw, r1_sem, r2_sem, r3_sem):
    batches, tokens, features = x_hbm.shape
    own_tokens = g_hbm.shape[1]
    blocks = g.shape[0]
    copy, tp = lax.axis_index("copy"), lax.axis_index("tp")
    z, y, x = copy // 16, (copy // 4) % 4, copy % 4
    chip, core = tp // 2, tp % 2

    def turn(v, by):
        return lax.rem(v + by, RING)

    def at(zz, yy, xx):
        return (zz * 16 + yy * 4 + xx, tp)

    pair = (copy, (1 - chip) * 2 + core)
    sibling = (copy, chip * 2 + 1 - core)
    own_rows = pl.ds(pl.multiple_of(tp * own_tokens, own_tokens), own_tokens)
    pair_rows = pl.ds(pl.multiple_of(pair[1] * own_tokens, own_tokens), own_tokens)

    barrier = pltpu.get_barrier_semaphore()
    partners = [pair, sibling]
    for d in (2, 1, 3):
        partners += [at(z, y, turn(x, d)), at(z, turn(y, d), x), at(turn(z, d), y, x)]
    for partner in partners:
        pl.semaphore_signal(barrier, 1, device_id=partner, device_id_type=MESH)

    loads = []
    for k in range(blocks):
        loads.append(pltpu.make_async_copy(
            g_hbm.at[:, :, pl.ds(k * CW, CW)], g.at[k, :, own_rows, :], g_sem.at[k]))
    w_load = pltpu.make_async_copy(w_hbm, wv, w_sem)
    x_loads = [pltpu.make_async_copy(x_hbm.at[m], xv.at[m], x_sem.at[m]) for m in range(batches)]
    for load in loads + [w_load] + x_loads:
        load.start()
    pl.semaphore_wait(barrier, len(partners))

    def send(src, dst, slot, recv, to):
        pltpu.make_async_remote_copy(src, dst, send_sem.at[slot], recv, device_id=to, device_id_type=MESH).start()

    def take(ref, sem):
        pltpu.make_async_copy(ref, ref, sem).wait()

    for k in range(blocks):
        loads[k].wait()
        own = g.at[k, :, own_rows, :]
        send(own, own, 0, rz.at[k], pair)
        send(own, own, 1, rc.at[k], sibling)
    w_load.wait()
    for d in (2, 1, 3):
        send(wv.at[pl.ds(0, HALF), :, turn(x, d)], rwx.at[d - 1], 3, rw.at[0], at(z, y, turn(x, d)))
        send(wv.at[pl.ds(HALF, HALF), turn(y, d)], rwy.at[d - 1], 3, rw.at[1], at(z, turn(y, d), x))

    for m in range(batches):
        x_loads[m].wait()

        def turn_tile(i, c, m=m):
            cols = pl.ds(pl.multiple_of(i * 256, 256), 256)
            xt[m, cols, :] = xv[m, :, cols].T
            return c

        lax.fori_loop(0, features // 256, turn_tile, 0)

    def relay(k):
        got = g.at[k, :, pair_rows, :]
        take(got, rz.at[k])
        send(got, got, 2, rr.at[k], sibling)

    def compute(k):
        got = g.at[k, :, own_rows, :]
        take(got, rc.at[k])
        take(got, rr.at[k])

        def tile(i):
            rows = pl.ds(i * 512, 512)
            total = None
            for m in range(batches):
                gradient = jnp.dot(xt[m, rows, :], g[k, m], preferred_element_type=jnp.float32)
                square = gradient * gradient
                total = square if total is None else total + square
            total = total.reshape(HALF, RING, RING, ROWS, CW)
            f[k, pl.ds(i * HALF, HALF)] = total
            high0, part0 = split(total[0])
            high1, part1 = split(total[1])
            e[k, i, 0] = high0
            e[k, i, 1] = high1
            e[k, i, 2] = (part0 * 16.0 + part1).astype(jnp.bfloat16)

        tile(0)
        for d in (2, 1, 3):
            send(e.at[k, 0, :, :, turn(x, d)], r1x.at[k, d - 1], 4, r1_sem.at[0, k],
                 at(z, y, turn(x, d)))
        tile(1)
        for d in (2, 1, 3):
            send(e.at[k, 1, :, turn(y, d)], r1y.at[k, d - 1], 5, r1_sem.at[1, k],
                 at(z, turn(y, d), x))

    def stage1(k):
        cols = pl.ds(pl.multiple_of(k * CW, CW), CW)

        def add(own_f, own_w, rf, rw_):
            fisher = own_f
            weighted = own_f * own_w.astype(jnp.float32)
            for d in range(RING - 1):
                parts = rf[k, d, 2].astype(jnp.float32)
                part0 = jnp.floor(parts * (1.0 / 16))
                theirs = jnp.stack([joined(rf[k, d, 0], part0), joined(rf[k, d, 1], parts - 16.0 * part0)])
                fisher = fisher + theirs
                weighted = weighted + theirs * rw_[d, :, :, :, cols].astype(jnp.float32)
            return weighted, fisher

        take(r1x.at[k], r1_sem.at[0, k])
        weighted, fisher = add(f[k, pl.ds(0, HALF), :, x], wv[pl.ds(0, HALF), :, x, :, cols], r1x, rwx)
        s2x[k, :, 0] = weighted
        s2x[k, :, 1] = fisher
        for d in (2, 1, 3):
            send(s2x.at[k, :, :, turn(y, d)], r2x.at[k, d - 1], 6, r2_sem.at[0, k], at(z, turn(y, d), x))
        take(r1y.at[k], r1_sem.at[1, k])
        weighted, fisher = add(f[k, pl.ds(HALF, HALF), y], wv[pl.ds(HALF, HALF), y, :, :, cols], r1y, rwy)
        s2y[k, :, 0] = weighted
        s2y[k, :, 1] = fisher
        for d in (2, 1, 3):
            send(s2y.at[k, :, :, turn(x, d)], r2y.at[k, d - 1], 7, r2_sem.at[1, k], at(z, y, turn(x, d)))

    def stage2(k):
        take(r2x.at[k], r2_sem.at[0, k])
        s3[k, pl.ds(0, HALF)] = s2x[k, :, :, y] + r2x[k, 0] + r2x[k, 1] + r2x[k, 2]
        take(r2y.at[k], r2_sem.at[1, k])
        s3[k, pl.ds(HALF, HALF)] = s2y[k, :, :, x] + r2y[k, 0] + r2y[k, 1] + r2y[k, 2]

    def send3(k):
        for d in (2, 1, 3):
            send(s3.at[k, turn(z, d)], r3.at[k, d - 1], 8, r3_sem.at[k], at(turn(z, d), y, x))

    def stage3(k):
        cols = pl.ds(pl.multiple_of(k * CW, CW), CW)
        take(r3.at[k], r3_sem.at[k])
        sums = (s3[k, z] + r3[k, 0] + r3[k, 1] + r3[k, 2]) * (1.0 / (batches * tokens))
        out_ref[:, :, cols] = sums

    def step(i, c):
        @pl.when(i < blocks)
        def _():
            relay(i)

        @pl.when(i == LAG1)
        def _():
            take(rwx, rw.at[0])
            take(rwy, rw.at[1])

        @pl.when(jnp.logical_and(i >= LAG1, i < blocks + LAG1))
        def _():
            stage1(i - LAG1)

        @pl.when(jnp.logical_and(i >= LAG2, i < blocks + LAG2))
        def _():
            stage2(i - LAG2)

        @pl.when(i == blocks)
        def _():
            lax.fori_loop(0, blocks - LAG2 + 1, lambda k, c: (send3(k), c)[1], 0)

        @pl.when(jnp.logical_and(i > blocks, i < blocks + LAG2))
        def _():
            send3(i - LAG2)

        @pl.when(i >= LAG3)
        def _():
            stage3(i - LAG3)

        @pl.when(i < blocks)
        def _():
            compute(i)

        return c

    lax.fori_loop(0, blocks + LAG3, step, 0)

    own = g.at[:, :, own_rows, :]
    for slot in range(3):
        take(own, send_sem.at[slot])
    take(rwx, send_sem.at[3])
    take(rwy, send_sem.at[3])
    for slot, ref in ((4, r1x), (5, r1y), (6, r2x), (7, r2y), (8, r3)):
        take(ref, send_sem.at[slot])


def local(layer_inputs, output_grads, value_weights):
    _, batches, tokens, _, features = layer_inputs.shape
    own_tokens, columns = output_grads.shape[2:]
    blocks = columns // CW
    f32, bf16 = jnp.float32, jnp.bfloat16
    dma = pltpu.SemaphoreType.DMA
    vmem = pltpu.VMEM
    sums = pl.pallas_call(
        kernel,
        out_shape=jax.ShapeDtypeStruct((2, ROWS, columns), f32),
        in_specs=[pl.BlockSpec(memory_space=pl.ANY)] * 3,
        out_specs=pl.BlockSpec(memory_space=pltpu.VMEM),
        scratch_shapes=[
            vmem((batches, tokens, features), bf16),
            vmem((batches, features, tokens), bf16),
            vmem((blocks, batches, tokens, CW), bf16),
            vmem((RING, RING, RING, ROWS, columns), bf16),
            vmem((blocks, RING, RING, RING, ROWS, CW), f32),
            vmem((blocks, HALF, 3, RING, RING, ROWS, CW), bf16),
            vmem((RING - 1, HALF, RING, ROWS, columns), bf16),
            vmem((RING - 1, HALF, RING, ROWS, columns), bf16),
            vmem((blocks, RING - 1, 3, RING, ROWS, CW), bf16),
            vmem((blocks, RING - 1, 3, RING, ROWS, CW), bf16),
            vmem((blocks, HALF, 2, RING, ROWS, CW), f32),
            vmem((blocks, HALF, 2, RING, ROWS, CW), f32),
            vmem((blocks, RING - 1, HALF, 2, ROWS, CW), f32),
            vmem((blocks, RING - 1, HALF, 2, ROWS, CW), f32),
            vmem((blocks, RING, 2, ROWS, CW), f32),
            vmem((blocks, RING - 1, 2, ROWS, CW), f32),
            dma((batches,)), dma((blocks,)), dma, dma((9,)),
            dma((blocks,)), dma((blocks,)), dma((blocks,)), dma((2,)),
            dma((2, blocks)), dma((2, blocks)), dma((blocks,)),
        ],
        compiler_params=pltpu.CompilerParams(
            collective_id=0, has_side_effects=True, vmem_limit_bytes=56 << 20
        ),
        cost_estimate=pl.CostEstimate(
            flops=2 * batches * tokens * features * columns, bytes_accessed=10 << 20, transcendentals=0
        ),
        name="fisher_merge",
    )(
        layer_inputs.reshape(batches, tokens, features),
        output_grads.reshape(batches, own_tokens, columns),
        value_weights.reshape(RING, RING, RING, ROWS, columns),
    )
    weighted, total = sums[:1], sums[1:]
    return (weighted / (total + EPSILON)).astype(bf16), total / lax.axis_size("copy")


def solution(mesh):
    return jax.shard_map(
        local,
        mesh=mesh,
        in_specs=(
            P("copy", None, None, "tp", None),
            P("copy", None, "tp", None),
            P("copy", "tp", None, None),
        ),
        out_specs=(P("tp", "copy", None), P("tp", "copy", None)),
        check_vma=False,
    )
```

```python
import jax
import jax.numpy as jnp
from jax import lax
from jax.experimental import pallas as pl
from jax.experimental.pallas import tpu as pltpu
from jax.sharding import PartitionSpec as P

EPSILON = 1e-6
RING = 4
HALF = RING // 2
ROWS = 16
CW = 128
LAG1, LAG2, LAG3 = 3, 5, 10
MESH = pl.DeviceIdType.MESH


def spacing(high):
    return (high * (1.0 + 1.01 / 256)).astype(jnp.bfloat16).astype(jnp.float32) - high


def split(value):
    high = value.astype(jnp.bfloat16)
    near = high.astype(jnp.float32)
    part = (value - near) * pl.reciprocal(jnp.maximum(spacing(near), 1e-30), approx=True)
    return high, jnp.clip(jnp.floor(part * 16.0 + 8.0), 0.0, 15.0)


def joined(high, sixteenths):
    near = high.astype(jnp.float32)
    return near + (sixteenths - 7.5) * (spacing(near) * (1.0 / 16))


def kernel(x_hbm, g_hbm, w_hbm, out_ref,
           xv, xt, g, wv, f, e, rwx, rwy, r1x, r1y, s2x, s2y, r2x, r2y, s3, r3,
           x_sem, g_sem, w_sem, send_sem, rz, rc, rr, rw, r1_sem, r2_sem, r3_sem):
    batches, tokens, features = x_hbm.shape
    own_tokens = g_hbm.shape[1]
    blocks = g.shape[0]
    copy, tp = lax.axis_index("copy"), lax.axis_index("tp")
    z, y, x = copy // 16, (copy // 4) % 4, copy % 4
    chip, core = tp // 2, tp % 2

    def turn(v, by):
        return lax.rem(v + by, RING)

    def at(zz, yy, xx):
        return (zz * 16 + yy * 4 + xx, tp)

    pair = (copy, (1 - chip) * 2 + core)
    sibling = (copy, chip * 2 + 1 - core)
    own_rows = pl.ds(pl.multiple_of(tp * own_tokens, own_tokens), own_tokens)
    pair_rows = pl.ds(pl.multiple_of(pair[1] * own_tokens, own_tokens), own_tokens)

    barrier = pltpu.get_barrier_semaphore()
    partners = [pair, sibling]
    for d in (2, 1, 3):
        partners += [at(z, y, turn(x, d)), at(z, turn(y, d), x), at(turn(z, d), y, x)]
    for partner in partners:
        pl.semaphore_signal(barrier, 1, device_id=partner, device_id_type=MESH)

    loads = []
    for k in range(blocks):
        loads.append(pltpu.make_async_copy(
            g_hbm.at[:, :, pl.ds(k * CW, CW)], g.at[k, :, own_rows, :], g_sem.at[k]))
    w_load = pltpu.make_async_copy(w_hbm, wv, w_sem)
    x_loads = [pltpu.make_async_copy(x_hbm.at[m], xv.at[m], x_sem.at[m]) for m in range(batches)]
    for load in loads + [w_load] + x_loads:
        load.start()
    pl.semaphore_wait(barrier, len(partners))

    def send(src, dst, slot, recv, to):
        pltpu.make_async_remote_copy(src, dst, send_sem.at[slot], recv, device_id=to, device_id_type=MESH).start()

    def take(ref, sem):
        pltpu.make_async_copy(ref, ref, sem).wait()

    for k in range(blocks):
        loads[k].wait()
        own = g.at[k, :, own_rows, :]
        send(own, own, 0, rz.at[k], pair)
        send(own, own, 1, rc.at[k], sibling)
    w_load.wait()
    for d in (2, 1, 3):
        send(wv.at[pl.ds(0, HALF), :, turn(x, d)], rwx.at[d - 1], 3, rw.at[0], at(z, y, turn(x, d)))
        send(wv.at[pl.ds(HALF, HALF), turn(y, d)], rwy.at[d - 1], 3, rw.at[1], at(z, turn(y, d), x))

    for m in range(batches):
        x_loads[m].wait()

        def turn_tile(i, c, m=m):
            cols = pl.ds(pl.multiple_of(i * 256, 256), 256)
            xt[m, cols, :] = xv[m, :, cols].T
            return c

        lax.fori_loop(0, features // 256, turn_tile, 0)

    def relay(k):
        got = g.at[k, :, pair_rows, :]
        take(got, rz.at[k])
        send(got, got, 2, rr.at[k], sibling)

    def compute(k):
        got = g.at[k, :, own_rows, :]
        take(got, rc.at[k])
        take(got, rr.at[k])

        def tile(i):
            rows = pl.ds(i * 512, 512)
            total = None
            for m in range(batches):
                gradient = jnp.dot(xt[m, rows, :], g[k, m], preferred_element_type=jnp.float32)
                square = gradient * gradient
                total = square if total is None else total + square
            total = total.reshape(HALF, RING, RING, ROWS, CW)
            f[k, pl.ds(i * HALF, HALF)] = total
            high0, part0 = split(total[0])
            high1, part1 = split(total[1])
            parts = (part0 * 16.0 + part1).astype(jnp.bfloat16)
            for to in range(RING):
                for kind, value in enumerate((high0, high1, parts)):
                    e[k, i, to, kind] = value[:, to] if i == 0 else value[to]

        tile(0)
        for d in (2, 1, 3):
            send(e.at[k, 0, turn(x, d)], r1x.at[k, d - 1], 4, r1_sem.at[0, k],
                 at(z, y, turn(x, d)))
        tile(1)
        for d in (2, 1, 3):
            send(e.at[k, 1, turn(y, d)], r1y.at[k, d - 1], 5, r1_sem.at[1, k],
                 at(z, turn(y, d), x))

    def stage1(k):
        cols = pl.ds(pl.multiple_of(k * CW, CW), CW)

        def add(own_f, own_w, rf, rw_):
            fisher = own_f
            weighted = own_f * own_w.astype(jnp.float32)
            for d in range(RING - 1):
                parts = rf[k, d, 2].astype(jnp.float32)
                part0 = jnp.floor(parts * (1.0 / 16))
                theirs = jnp.stack([joined(rf[k, d, 0], part0), joined(rf[k, d, 1], parts - 16.0 * part0)])
                fisher = fisher + theirs
                weighted = weighted + theirs * rw_[d, :, :, :, cols].astype(jnp.float32)
            return weighted, fisher

        take(r1x.at[k], r1_sem.at[0, k])
        weighted, fisher = add(f[k, pl.ds(0, HALF), :, x], wv[pl.ds(0, HALF), :, x, :, cols], r1x, rwx)
        for to in range(RING):
            s2x[k, to, :, 0] = weighted[:, to]
            s2x[k, to, :, 1] = fisher[:, to]
        for d in (2, 1, 3):
            send(s2x.at[k, turn(y, d)], r2x.at[k, d - 1], 6, r2_sem.at[0, k], at(z, turn(y, d), x))
        take(r1y.at[k], r1_sem.at[1, k])
        weighted, fisher = add(f[k, pl.ds(HALF, HALF), y], wv[pl.ds(HALF, HALF), y, :, :, cols], r1y, rwy)
        for to in range(RING):
            s2y[k, to, :, 0] = weighted[:, to]
            s2y[k, to, :, 1] = fisher[:, to]
        for d in (2, 1, 3):
            send(s2y.at[k, turn(x, d)], r2y.at[k, d - 1], 7, r2_sem.at[1, k], at(z, y, turn(x, d)))

    def stage2(k):
        take(r2x.at[k], r2_sem.at[0, k])
        s3[k, pl.ds(0, HALF)] = s2x[k, y] + r2x[k, 0] + r2x[k, 1] + r2x[k, 2]
        take(r2y.at[k], r2_sem.at[1, k])
        s3[k, pl.ds(HALF, HALF)] = s2y[k, x] + r2y[k, 0] + r2y[k, 1] + r2y[k, 2]

    def send3(k):
        for d in (2, 1, 3):
            send(s3.at[k, turn(z, d)], r3.at[k, d - 1], 8, r3_sem.at[k], at(turn(z, d), y, x))

    def stage3(k):
        cols = pl.ds(pl.multiple_of(k * CW, CW), CW)
        take(r3.at[k], r3_sem.at[k])
        sums = (s3[k, z] + r3[k, 0] + r3[k, 1] + r3[k, 2]) * (1.0 / (batches * tokens))
        out_ref[:, :, cols] = sums

    def step(i, c):
        @pl.when(i < blocks)
        def _():
            relay(i)

        @pl.when(i == LAG1)
        def _():
            take(rwx, rw.at[0])
            take(rwy, rw.at[1])

        @pl.when(jnp.logical_and(i >= LAG1, i < blocks + LAG1))
        def _():
            stage1(i - LAG1)

        @pl.when(jnp.logical_and(i >= LAG2, i < blocks + LAG2))
        def _():
            stage2(i - LAG2)

        @pl.when(i == blocks)
        def _():
            lax.fori_loop(0, blocks - LAG2 + 1, lambda k, c: (send3(k), c)[1], 0)

        @pl.when(jnp.logical_and(i > blocks, i < blocks + LAG2))
        def _():
            send3(i - LAG2)

        @pl.when(i >= LAG3)
        def _():
            stage3(i - LAG3)

        @pl.when(i < blocks)
        def _():
            compute(i)

        return c

    lax.fori_loop(0, blocks + LAG3, step, 0)

    own = g.at[:, :, own_rows, :]
    for slot in range(3):
        take(own, send_sem.at[slot])
    take(rwx, send_sem.at[3])
    take(rwy, send_sem.at[3])
    for slot, ref in ((4, r1x), (5, r1y), (6, r2x), (7, r2y), (8, r3)):
        take(ref, send_sem.at[slot])


def local(layer_inputs, output_grads, value_weights):
    _, batches, tokens, _, features = layer_inputs.shape
    own_tokens, columns = output_grads.shape[2:]
    blocks = columns // CW
    f32, bf16 = jnp.float32, jnp.bfloat16
    dma = pltpu.SemaphoreType.DMA
    vmem = pltpu.VMEM
    sums = pl.pallas_call(
        kernel,
        out_shape=jax.ShapeDtypeStruct((2, ROWS, columns), f32),
        in_specs=[pl.BlockSpec(memory_space=pl.ANY)] * 3,
        out_specs=pl.BlockSpec(memory_space=pltpu.VMEM),
        scratch_shapes=[
            vmem((batches, tokens, features), bf16),
            vmem((batches, features, tokens), bf16),
            vmem((blocks, batches, tokens, CW), bf16),
            vmem((RING, RING, RING, ROWS, columns), bf16),
            vmem((blocks, RING, RING, RING, ROWS, CW), f32),
            vmem((blocks, HALF, RING, 3, RING, ROWS, CW), bf16),
            vmem((RING - 1, HALF, RING, ROWS, columns), bf16),
            vmem((RING - 1, HALF, RING, ROWS, columns), bf16),
            vmem((blocks, RING - 1, 3, RING, ROWS, CW), bf16),
            vmem((blocks, RING - 1, 3, RING, ROWS, CW), bf16),
            vmem((blocks, RING, HALF, 2, ROWS, CW), f32),
            vmem((blocks, RING, HALF, 2, ROWS, CW), f32),
            vmem((blocks, RING - 1, HALF, 2, ROWS, CW), f32),
            vmem((blocks, RING - 1, HALF, 2, ROWS, CW), f32),
            vmem((blocks, RING, 2, ROWS, CW), f32),
            vmem((blocks, RING - 1, 2, ROWS, CW), f32),
            dma((batches,)), dma((blocks,)), dma, dma((9,)),
            dma((blocks,)), dma((blocks,)), dma((blocks,)), dma((2,)),
            dma((2, blocks)), dma((2, blocks)), dma((blocks,)),
        ],
        compiler_params=pltpu.CompilerParams(
            collective_id=0, has_side_effects=True, vmem_limit_bytes=56 << 20
        ),
        cost_estimate=pl.CostEstimate(
            flops=2 * batches * tokens * features * columns, bytes_accessed=10 << 20, transcendentals=0
        ),
        name="fisher_merge",
    )(
        layer_inputs.reshape(batches, tokens, features),
        output_grads.reshape(batches, own_tokens, columns),
        value_weights.reshape(RING, RING, RING, ROWS, columns),
    )
    weighted, total = sums[:1], sums[1:]
    return (weighted / (total + EPSILON)).astype(bf16), total / lax.axis_size("copy")


def solution(mesh):
    return jax.shard_map(
        local,
        mesh=mesh,
        in_specs=(
            P("copy", None, None, "tp", None),
            P("copy", None, "tp", None),
            P("copy", "tp", None, None),
        ),
        out_specs=(P("tp", "copy", None), P("tp", "copy", None)),
        check_vma=False,
    )
```

```python
import jax
import jax.numpy as jnp
from jax import lax
from jax.experimental import pallas as pl
from jax.experimental.pallas import tpu as pltpu
from jax.sharding import PartitionSpec as P

EPSILON = 1e-6
RING = 4
HALF = RING // 2
ROWS = 16
CW = 128
LAG1, LAG2, LAG3 = 3, 5, 10
MESH = pl.DeviceIdType.MESH


def spacing(high):
    return (high * (1.0 + 1.01 / 256)).astype(jnp.bfloat16).astype(jnp.float32) - high


def split(value):
    high = value.astype(jnp.bfloat16)
    near = high.astype(jnp.float32)
    part = (value - near) * pl.reciprocal(jnp.maximum(spacing(near), 1e-37), approx=True)
    return high, jnp.clip(jnp.floor(part * 16.0 + 8.0), 0.0, 15.0)


def joined(high, sixteenths):
    near = high.astype(jnp.float32)
    return near + (sixteenths - 7.5) * (spacing(near) * (1.0 / 16))


def kernel(x_hbm, g_hbm, w_hbm, out_ref,
           xv, xt, g, wv, f, e, rwx, rwy, r1x, r1y, s2x, s2y, r2x, r2y, s3, r3,
           x_sem, g_sem, w_sem, send_sem, rz, rc, rr, rw, r1_sem, r2_sem, r3_sem):
    batches, tokens, features = x_hbm.shape
    own_tokens = g_hbm.shape[1]
    blocks = g.shape[0]
    copy, tp = lax.axis_index("copy"), lax.axis_index("tp")
    z, y, x = copy // 16, (copy // 4) % 4, copy % 4
    chip, core = tp // 2, tp % 2

    def turn(v, by):
        return lax.rem(v + by, RING)

    def at(zz, yy, xx):
        return (zz * 16 + yy * 4 + xx, tp)

    pair = (copy, (1 - chip) * 2 + core)
    sibling = (copy, chip * 2 + 1 - core)
    own_rows = pl.ds(pl.multiple_of(tp * own_tokens, own_tokens), own_tokens)
    pair_rows = pl.ds(pl.multiple_of(pair[1] * own_tokens, own_tokens), own_tokens)

    barrier = pltpu.get_barrier_semaphore()
    partners = [pair, sibling]
    for d in (2, 1, 3):
        partners += [at(z, y, turn(x, d)), at(z, turn(y, d), x), at(turn(z, d), y, x)]
    for partner in partners:
        pl.semaphore_signal(barrier, 1, device_id=partner, device_id_type=MESH)

    loads = []
    for k in range(blocks):
        loads.append(pltpu.make_async_copy(
            g_hbm.at[:, :, pl.ds(k * CW, CW)], g.at[k, :, own_rows, :], g_sem.at[k]))
    w_load = pltpu.make_async_copy(w_hbm, wv, w_sem)
    x_loads = [pltpu.make_async_copy(x_hbm.at[m], xv.at[m], x_sem.at[m]) for m in range(batches)]
    for load in loads + [w_load] + x_loads:
        load.start()
    pl.semaphore_wait(barrier, len(partners))

    def send(src, dst, slot, recv, to):
        pltpu.make_async_remote_copy(src, dst, send_sem.at[slot], recv, device_id=to, device_id_type=MESH).start()

    def take(ref, sem):
        pltpu.make_async_copy(ref, ref, sem).wait()

    for k in range(blocks):
        loads[k].wait()
        own = g.at[k, :, own_rows, :]
        send(own, own, 0, rz.at[k], pair)
        send(own, own, 1, rc.at[k], sibling)
    w_load.wait()
    for d in (2, 1, 3):
        send(wv.at[pl.ds(0, HALF), :, turn(x, d)], rwx.at[d - 1], 3, rw.at[0], at(z, y, turn(x, d)))
        send(wv.at[pl.ds(HALF, HALF), turn(y, d)], rwy.at[d - 1], 3, rw.at[1], at(z, turn(y, d), x))

    for m in range(batches):
        x_loads[m].wait()

        def turn_tile(i, c, m=m):
            cols = pl.ds(pl.multiple_of(i * 256, 256), 256)
            xt[m, cols, :] = xv[m, :, cols].T
            return c

        lax.fori_loop(0, features // 256, turn_tile, 0)

    def relay(k):
        got = g.at[k, :, pair_rows, :]
        take(got, rz.at[k])
        send(got, got, 2, rr.at[k], sibling)

    def compute(k):
        got = g.at[k, :, own_rows, :]
        take(got, rc.at[k])
        take(got, rr.at[k])

        def tile(i):
            rows = pl.ds(i * 512, 512)
            total = None
            for m in range(batches):
                gradient = jnp.dot(xt[m, rows, :], g[k, m], preferred_element_type=jnp.float32)
                square = gradient * gradient
                total = square if total is None else total + square
            total = total.reshape(HALF, RING, RING, ROWS, CW)
            f[k, pl.ds(i * HALF, HALF)] = total
            high0, part0 = split(total[0])
            high1, part1 = split(total[1])
            parts = (part0 * 16.0 + part1).astype(jnp.bfloat16)
            for to in range(RING):
                for kind, value in enumerate((high0, high1, parts)):
                    e[k, i, to, kind] = value[:, to] if i == 0 else value[to]

        tile(0)
        for d in (2, 1, 3):
            send(e.at[k, 0, turn(x, d)], r1x.at[k, d - 1], 4, r1_sem.at[0, k],
                 at(z, y, turn(x, d)))
        tile(1)
        for d in (2, 1, 3):
            send(e.at[k, 1, turn(y, d)], r1y.at[k, d - 1], 5, r1_sem.at[1, k],
                 at(z, turn(y, d), x))

    def stage1(k):
        cols = pl.ds(pl.multiple_of(k * CW, CW), CW)

        def add(own_f, own_w, rf, rw_):
            fisher = own_f
            weighted = own_f * own_w.astype(jnp.float32)
            for d in range(RING - 1):
                parts = rf[k, d, 2].astype(jnp.float32)
                part0 = jnp.floor(parts * (1.0 / 16))
                theirs = jnp.stack([joined(rf[k, d, 0], part0), joined(rf[k, d, 1], parts - 16.0 * part0)])
                fisher = fisher + theirs
                weighted = weighted + theirs * rw_[d, :, :, :, cols].astype(jnp.float32)
            return weighted, fisher

        take(r1x.at[k], r1_sem.at[0, k])
        weighted, fisher = add(f[k, pl.ds(0, HALF), :, x], wv[pl.ds(0, HALF), :, x, :, cols], r1x, rwx)
        for to in range(RING):
            s2x[k, to, :, 0] = weighted[:, to]
            s2x[k, to, :, 1] = fisher[:, to]
        for d in (2, 1, 3):
            send(s2x.at[k, turn(y, d)], r2x.at[k, d - 1], 6, r2_sem.at[0, k], at(z, turn(y, d), x))
        take(r1y.at[k], r1_sem.at[1, k])
        weighted, fisher = add(f[k, pl.ds(HALF, HALF), y], wv[pl.ds(HALF, HALF), y, :, :, cols], r1y, rwy)
        for to in range(RING):
            s2y[k, to, :, 0] = weighted[:, to]
            s2y[k, to, :, 1] = fisher[:, to]
        for d in (2, 1, 3):
            send(s2y.at[k, turn(x, d)], r2y.at[k, d - 1], 7, r2_sem.at[1, k], at(z, y, turn(x, d)))

    def stage2(k):
        take(r2x.at[k], r2_sem.at[0, k])
        s3[k, pl.ds(0, HALF)] = s2x[k, y] + r2x[k, 0] + r2x[k, 1] + r2x[k, 2]
        take(r2y.at[k], r2_sem.at[1, k])
        s3[k, pl.ds(HALF, HALF)] = s2y[k, x] + r2y[k, 0] + r2y[k, 1] + r2y[k, 2]

    def send3(k):
        for d in (2, 1, 3):
            send(s3.at[k, turn(z, d)], r3.at[k, d - 1], 8, r3_sem.at[k], at(turn(z, d), y, x))

    def stage3(k):
        cols = pl.ds(pl.multiple_of(k * CW, CW), CW)
        take(r3.at[k], r3_sem.at[k])
        sums = (s3[k, z] + r3[k, 0] + r3[k, 1] + r3[k, 2]) * (1.0 / (batches * tokens))
        out_ref[:, :, cols] = sums

    def step(i, c):
        @pl.when(i < blocks)
        def _():
            relay(i)

        @pl.when(i == LAG1)
        def _():
            take(rwx, rw.at[0])
            take(rwy, rw.at[1])

        @pl.when(jnp.logical_and(i >= LAG1, i < blocks + LAG1))
        def _():
            stage1(i - LAG1)

        @pl.when(jnp.logical_and(i >= LAG2, i < blocks + LAG2))
        def _():
            stage2(i - LAG2)

        @pl.when(i == blocks)
        def _():
            lax.fori_loop(0, blocks - LAG2 + 1, lambda k, c: (send3(k), c)[1], 0)

        @pl.when(jnp.logical_and(i > blocks, i < blocks + LAG2))
        def _():
            send3(i - LAG2)

        @pl.when(i >= LAG3)
        def _():
            stage3(i - LAG3)

        @pl.when(i < blocks)
        def _():
            compute(i)

        return c

    lax.fori_loop(0, blocks + LAG3, step, 0)

    own = g.at[:, :, own_rows, :]
    for slot in range(3):
        take(own, send_sem.at[slot])
    take(rwx, send_sem.at[3])
    take(rwy, send_sem.at[3])
    for slot, ref in ((4, r1x), (5, r1y), (6, r2x), (7, r2y), (8, r3)):
        take(ref, send_sem.at[slot])


def local(layer_inputs, output_grads, value_weights):
    _, batches, tokens, _, features = layer_inputs.shape
    own_tokens, columns = output_grads.shape[2:]
    blocks = columns // CW
    f32, bf16 = jnp.float32, jnp.bfloat16
    dma = pltpu.SemaphoreType.DMA
    vmem = pltpu.VMEM
    sums = pl.pallas_call(
        kernel,
        out_shape=jax.ShapeDtypeStruct((2, ROWS, columns), f32),
        in_specs=[pl.BlockSpec(memory_space=pl.ANY)] * 3,
        out_specs=pl.BlockSpec(memory_space=pltpu.VMEM),
        scratch_shapes=[
            vmem((batches, tokens, features), bf16),
            vmem((batches, features, tokens), bf16),
            vmem((blocks, batches, tokens, CW), bf16),
            vmem((RING, RING, RING, ROWS, columns), bf16),
            vmem((blocks, RING, RING, RING, ROWS, CW), f32),
            vmem((blocks, HALF, RING, 3, RING, ROWS, CW), bf16),
            vmem((RING - 1, HALF, RING, ROWS, columns), bf16),
            vmem((RING - 1, HALF, RING, ROWS, columns), bf16),
            vmem((blocks, RING - 1, 3, RING, ROWS, CW), bf16),
            vmem((blocks, RING - 1, 3, RING, ROWS, CW), bf16),
            vmem((blocks, RING, HALF, 2, ROWS, CW), f32),
            vmem((blocks, RING, HALF, 2, ROWS, CW), f32),
            vmem((blocks, RING - 1, HALF, 2, ROWS, CW), f32),
            vmem((blocks, RING - 1, HALF, 2, ROWS, CW), f32),
            vmem((blocks, RING, 2, ROWS, CW), f32),
            vmem((blocks, RING - 1, 2, ROWS, CW), f32),
            dma((batches,)), dma((blocks,)), dma, dma((9,)),
            dma((blocks,)), dma((blocks,)), dma((blocks,)), dma((2,)),
            dma((2, blocks)), dma((2, blocks)), dma((blocks,)),
        ],
        compiler_params=pltpu.CompilerParams(
            collective_id=0, has_side_effects=True, vmem_limit_bytes=56 << 20
        ),
        cost_estimate=pl.CostEstimate(
            flops=2 * batches * tokens * features * columns, bytes_accessed=10 << 20, transcendentals=0
        ),
        name="fisher_merge",
    )(
        layer_inputs.reshape(batches, tokens, features),
        output_grads.reshape(batches, own_tokens, columns),
        value_weights.reshape(RING, RING, RING, ROWS, columns),
    )
    weighted, total = sums[:1], sums[1:]
    return (weighted / (total + EPSILON)).astype(bf16), total / lax.axis_size("copy")


def solution(mesh):
    return jax.shard_map(
        local,
        mesh=mesh,
        in_specs=(
            P("copy", None, None, "tp", None),
            P("copy", None, "tp", None),
            P("copy", "tp", None, None),
        ),
        out_specs=(P("tp", "copy", None), P("tp", "copy", None)),
        check_vma=False,
    )
```
